32 devices in a mesh: replica: 16 (over z, y, x), tensor: 2 (over core).
Axes of the slice: x: 2, y: 2, z: 4, core: 2. Of those that a mesh axis runs over, the one named last changes fastest.
Arguments:
- tokens: bfloat16 [32768, 768], P('replica'), may hold values from -6 to 6
- lengths: int32 [64], P('replica'), may hold values from 128 to 512, as said below
- w_qkv: bfloat16 [3, 768, 768], P(None, None, 'tensor'), may hold values from -0.21875 to 0.21875
- qv_bias: bfloat16 [2, 768], P(None, 'tensor'), may hold values from -3 to 3
- w_out: bfloat16 [768, 768], P('tensor'), may hold values from -1.25 to 1.25
- out_bias: bfloat16 [768], replicated, may hold values from -3 to 3
- ln1_gain: bfloat16 [768], replicated, may hold values from 0.5 to 1.5
- ln1_bias: bfloat16 [768], replicated, may hold values from -3 to 3
- w_in: bfloat16 [768, 3072], P(None, 'tensor'), may hold values from -0.21875 to 0.21875
- in_bias: bfloat16 [3072], P('tensor'), may hold values from -3 to 3
- w_down: bfloat16 [3072, 768], P('tensor'), may hold values from -0.109375 to 0.109375
- down_bias: bfloat16 [768], replicated, may hold values from -3 to 3
- ln2_gain: bfloat16 [768], replicated, may hold values from 0.5 to 1.5
- ln2_bias: bfloat16 [768], replicated, may hold values from -3 to 3
- cotangent: bfloat16 [32768, 768], P(('replica', 'tensor')), may hold values from -6 to 6
Outputs:
- mixed_out: bfloat16 [32768, 768], P(('replica', 'tensor'))
- input_grad: float32 [32768, 768], P(('replica', 'tensor'))
- grad_w_qkv: float32 [3, 768, 768], P(None, None, 'tensor')
- grad_qv_bias: float32 [2, 768], P(None, 'tensor')
- grad_w_out: float32 [768, 768], P('tensor')
- grad_out_bias: float32 [768], replicated
- grad_ln1_gain: float32 [768], replicated
- grad_ln1_bias: float32 [768], replicated
- grad_w_in: float32 [768, 3072], P(None, 'tensor')
- grad_in_bias: float32 [3072], P('tensor')
- grad_w_down: float32 [3072, 768], P('tensor')
- grad_down_bias: float32 [768], replicated
- grad_ln2_gain: float32 [768], replicated
- grad_ln2_bias: float32 [768], replicated
The draws below stay inside these ranges and needn't reach their ends.
Inputs may be any that keep to these rules, and one draw needn't show every extreme that they name: `lengths`: valid tokens of each sequence; keys at or past a sequence's length are masked; some sequence is full and some has exactly a quarter of 512.
All inputs are finite; a program needn't handle non-finite values.
Results may differ from the reference program's by a relative error of at most 0.018.
The reference program's roundings to bfloat16 on the way count: a program that leaves them out, or rounds other values in their place, can miss the bound.
Values may be sent and summed in bfloat16 or wider, within the bound.
A program may use at most 192 MiB of HBM per device.

```python
import jax
import jax.numpy as jnp
from jax import lax

D = 768
HEADS = 12
HD = 64
FF = 3072
LEN = 512
SEQ_DEV = 4
SEQS = 64
TOKENS = 32768
N_REPLICA = 16


def draw_lengths(key, part):
    key = jax.random.fold_in(key, 7)
    first_key, second_key = jax.random.split(key)
    drawn = jax.random.randint(first_key, (SEQS,), LEN // 4, LEN + 1)
    picked = jax.random.randint(second_key, (), 0, SEQS)
    drawn = drawn.at[picked].set(LEN)
    drawn = drawn.at[(picked + 1) % SEQS].set(LEN // 4)
    return drawn.astype(jnp.int32)


def levels(rng, dims, cuts, smallest, high):
    gain, own = 1.0, jax.random.fold_in(rng, 6)
    for position, shards_of in cuts:
        steps = jnp.exp(jax.random.uniform(jax.random.fold_in(own, position), (shards_of,), jnp.float32, smallest / len(cuts), high / len(cuts)))
        gain = gain * jnp.repeat(steps, dims[position] // shards_of).reshape([-1 if axis == position else 1 for axis in range(len(dims))])
    return gain


def gaussian(key, dims, spread, reach, cuts=(), kind=jnp.bfloat16):
    entries = spread * jax.random.normal(key, dims, jnp.float32)
    if cuts:
        entries = entries * levels(key, dims, cuts, -0.22, 0.18)
    return jnp.clip(entries, -reach, reach).astype(kind)


def setup_inputs(seed: int = 0) -> dict:
    streams_of = jax.random.split(jax.random.key(seed), 16)
    return {
        "tokens": gaussian(streams_of[0], (TOKENS, D), 1.0, 6.0, ((0, 16),)),
        "lengths": draw_lengths(jax.random.fold_in(streams_of[15], 71), 0),
        "w_qkv": gaussian(streams_of[2], (3, D, D), D ** -0.5, 0.21875, ((2, 2),)),
        "qv_bias": gaussian(streams_of[3], (2, D), 0.5, 3.0, ((1, 2),)),
        "w_out": gaussian(streams_of[4], (D, D), (D // 32) ** -0.5, 1.25, ((0, 2),)),
        "out_bias": gaussian(streams_of[5], (D,), 0.5, 3.0),
        "ln1_gain": jnp.clip(1.0 + 0.1 * jax.random.normal(streams_of[6], (D,), jnp.float32), 0.5, 1.5).astype(jnp.bfloat16),
        "ln1_bias": gaussian(streams_of[7], (D,), 0.5, 3.0),
        "w_in": gaussian(streams_of[8], (D, FF), D ** -0.5, 0.21875, ((1, 2),)),
        "in_bias": gaussian(streams_of[9], (FF,), 0.5, 3.0, ((0, 2),)),
        "w_down": gaussian(streams_of[10], (FF, D), FF ** -0.5, 0.109375, ((0, 2),)),
        "down_bias": gaussian(streams_of[11], (D,), 0.5, 3.0),
        "ln2_gain": jnp.clip(1.0 + 0.1 * jax.random.normal(streams_of[12], (D,), jnp.float32), 0.5, 1.5).astype(jnp.bfloat16),
        "ln2_bias": gaussian(streams_of[13], (D,), 0.5, 3.0),
        "cotangent": gaussian(streams_of[14], (TOKENS, D), 1.0, 6.0, ((0, 32),)),
    }


norm_eps = 1e-06

@jax.custom_vjp
def low(v):
    return lax.optimization_barrier(v.astype(jnp.bfloat16)).astype(jnp.float32)

@jax.custom_vjp
def low_back(v):
    return v

def low_keep(v):
    return (low(v), None)

def low_pass(kept, grad):
    return (grad,)

def back_keep(v):
    return (v, None)

def back_low(kept, grad):
    return (low(grad),)
low.defvjp(low_keep, low_pass)
low_back.defvjp(back_keep, back_low)

def matmul_high(left, right):
    return jnp.dot(left, right, precision=lax.Precision.HIGHEST)

def norm_rows(values, gain_vec, bias_vec):
    centered = values - lax.optimization_barrier(jnp.mean(values, axis=-1, keepdims=True))
    factor = lax.rsqrt(lax.optimization_barrier(jnp.mean(centered * centered, axis=-1, keepdims=True)) + norm_eps)
    return centered * factor * gain_vec + bias_vec

def attend_one(block):
    q_block, k_block, v_block, seq_length = block
    scores = jnp.einsum('qhd,khd->hqk', q_block, k_block, precision=lax.Precision.HIGHEST) * HD ** (-0.5)
    scores = low_back(scores)
    places = jnp.arange(q_block.shape[0], dtype=jnp.int32)
    scores = jnp.where(places[None, None, :] < seq_length, scores, -1000000000.0)
    prob_rows = jax.nn.softmax(scores, axis=-1)
    return jnp.einsum('hqk,khd->qhd', low(prob_rows), v_block, precision=lax.Precision.HIGHEST)

def layer_forward(inputs, w_qkv, qv_bias, w_out, out_bias, ln1_gain, ln1_bias, w_in, in_bias, w_down, down_bias, ln2_gain, ln2_bias, lengths):
    row_count = inputs.shape[0]
    seq_count = lengths.shape[0]
    shape4 = (seq_count, row_count // seq_count, HEADS, HD)
    queries = low(low_back(matmul_high(inputs, w_qkv[0]) + qv_bias[0]))
    keys_all = low(low_back(matmul_high(inputs, w_qkv[1])))
    values_all = low(low_back(matmul_high(inputs, w_qkv[2]) + qv_bias[1]))
    attended = lax.map(jax.checkpoint(attend_one), (queries.reshape(shape4), keys_all.reshape(shape4), values_all.reshape(shape4), lengths))
    attended = low(low_back(attended.reshape(row_count, D)))
    attn_sum = low_back(matmul_high(attended, w_out)) + out_bias
    hidden = norm_rows(inputs + attn_sum, ln1_gain, ln1_bias)
    inner = low_back(matmul_high(low(hidden), w_in)) + in_bias
    activated = low(jax.nn.gelu(inner, approximate=False))
    ffn_sum = low_back(matmul_high(activated, w_down)) + down_bias
    return norm_rows(hidden + ffn_sum, ln2_gain, ln2_bias)

def reference(tokens, lengths, w_qkv, qv_bias, w_out, out_bias, ln1_gain, ln1_bias, w_in, in_bias, w_down, down_bias, ln2_gain, ln2_bias, cotangent):
    params = tuple((param_arr.astype(jnp.float32) for param_arr in (w_qkv, qv_bias, w_out, out_bias, ln1_gain, ln1_bias, w_in, in_bias, w_down, down_bias, ln2_gain, ln2_bias)))
    row_count = SEQ_DEV * LEN
    inputs = tokens.astype(jnp.float32).reshape(N_REPLICA, row_count, D)
    grads_in = cotangent.astype(jnp.float32).reshape(N_REPLICA, row_count, D)
    seq_lengths = lengths.astype(jnp.int32).reshape(N_REPLICA, SEQ_DEV)

    def one_group(totals, block):
        group_in, group_len, group_grad = block

        def forward_part(group_inputs, *weights):
            return layer_forward(group_inputs, *weights, group_len)
        outputs, pull_back = jax.vjp(forward_part, group_in, *params)
        pulled = pull_back(group_grad)
        totals = tuple((running + new_grad for running, new_grad in zip(totals, pulled[1:])))
        return (totals, (outputs.astype(jnp.bfloat16), pulled[0]))
    initial = tuple((jnp.zeros_like(param_arr) for param_arr in params))
    totals, (mixed, grad_rows) = lax.scan(one_group, initial, (inputs, seq_lengths, grads_in))
    mixed = mixed.reshape(TOKENS, D)
    grad_rows = grad_rows.reshape(TOKENS, D)
    return (mixed, grad_rows, totals[0], totals[1], totals[2], totals[3], totals[4], totals[5], totals[6], totals[7], totals[8], totals[9], totals[10], totals[11])
```

```python
import functools

import jax
import jax.numpy as jnp
from jax import lax
from jax.experimental import pallas as pl
from jax.experimental.pallas import tpu as pltpu
from jax.sharding import PartitionSpec as P

HD = 64
norm_eps = 1e-06
f32 = jnp.float32
bf16 = jnp.bfloat16
VMEM_BYTES = 48 * 1024 * 1024


def dot_of(left, right, left_dim, right_dim):
    return lax.dot_general(
        left, right, (((left_dim,), (right_dim,)), ((), ())), preferred_element_type=f32
    )


def scores_of(keys, queries, length):
    scores = dot_of(keys, queries, 1, 1)
    places = lax.broadcasted_iota(jnp.int32, scores.shape, 0)
    return jnp.where(places < length, scores, -1000000000.0)


def forward_kernel(width, lengths_ref, qkv_ref, out_ref, lse_ref):
    length = lengths_ref[pl.program_id(0)]
    pair = 2 * HD
    for start in range(0, width, pair):
        both = []
        for head in range(start // HD, start // HD + 2):
            at = head * HD
            queries = qkv_ref[:, at : at + HD] * jnp.asarray(HD**-0.5, bf16)
            keys = qkv_ref[:, width + at : width + at + HD]
            values = qkv_ref[:, 2 * width + at : 2 * width + at + HD]
            scores = scores_of(keys, queries, length)
            top = jnp.max(scores, axis=0, keepdims=True)
            weights = jnp.exp(scores - top)
            total = jnp.sum(weights, axis=0, keepdims=True)
            probs = (weights * (1.0 / total)).astype(bf16)
            lse_ref[0, head : head + 1, :] = top + jnp.log(total)
            both.append(dot_of(values, probs, 0, 0))
        out_ref[:, start : start + pair] = jnp.concatenate(both, axis=0).T.astype(bf16)


def backward_kernel(width, lengths_ref, qkv_ref, lse_ref, grad_ref, out_ref):
    length = lengths_ref[pl.program_id(0)]
    pair = 2 * HD
    factor = HD**-0.5
    for start in range(0, width, pair):
        grad_q, grad_k, grad_v = [], [], []
        for head in range(start // HD, start // HD + 2):
            at = head * HD
            queries = qkv_ref[:, at : at + HD] * jnp.asarray(factor, bf16)
            keys = qkv_ref[:, width + at : width + at + HD]
            values = qkv_ref[:, 2 * width + at : 2 * width + at + HD]
            grads = grad_ref[:, at : at + HD]
            scores = scores_of(keys, queries, length)
            probs = jnp.exp(scores - lse_ref[0, head : head + 1, :])
            grad_probs = dot_of(values, grads, 1, 1)
            delta = jnp.sum(grad_probs * probs, axis=0, keepdims=True)
            grad_scores = (probs * (grad_probs - delta)).astype(bf16)
            grad_q.append(dot_of(keys, grad_scores, 0, 0) * factor)
            grad_k.append(dot_of(grad_scores, queries, 1, 0))
            grad_v.append(dot_of(probs.astype(bf16), grads, 1, 0))
        out_ref[:, start : start + pair] = jnp.concatenate(grad_q, axis=0).T.astype(bf16)
        at = width + start
        out_ref[:, at : at + pair] = jnp.concatenate(grad_k, axis=1).astype(bf16)
        at = 2 * width + start
        out_ref[:, at : at + pair] = jnp.concatenate(grad_v, axis=1).astype(bf16)


def attend(lengths, qkv):
    seqs = lengths.shape[0]
    rows, width = qkv.shape[0] // seqs, qkv.shape[1] // 3
    heads = width // HD
    work = seqs * heads * rows * rows
    return pl.pallas_call(
        functools.partial(forward_kernel, width),
        grid_spec=pltpu.PrefetchScalarGridSpec(
            num_scalar_prefetch=1,
            grid=(seqs,),
            in_specs=[pl.BlockSpec((rows, 3 * width), lambda s, lens: (s, 0))],
            out_specs=[
                pl.BlockSpec((rows, width), lambda s, lens: (s, 0)),
                pl.BlockSpec((1, heads, rows), lambda s, lens: (s, 0, 0)),
            ],
        ),
        out_shape=[
            jax.ShapeDtypeStruct((seqs * rows, width), bf16),
            jax.ShapeDtypeStruct((seqs, heads, rows), f32),
        ],
        compiler_params=pltpu.CompilerParams(vmem_limit_bytes=VMEM_BYTES),
        cost_estimate=pl.CostEstimate(
            flops=4 * work * HD, bytes_accessed=8 * seqs * rows * width, transcendentals=work
        ),
    )(lengths, qkv)


def attend_back(lengths, qkv, lse, grads):
    seqs = lengths.shape[0]
    rows, width = qkv.shape[0] // seqs, qkv.shape[1] // 3
    heads = width // HD
    work = seqs * heads * rows * rows
    return pl.pallas_call(
        functools.partial(backward_kernel, width),
        grid_spec=pltpu.PrefetchScalarGridSpec(
            num_scalar_prefetch=1,
            grid=(seqs,),
            in_specs=[
                pl.BlockSpec((rows, 3 * width), lambda s, lens: (s, 0)),
                pl.BlockSpec((1, heads, rows), lambda s, lens: (s, 0, 0)),
                pl.BlockSpec((rows, width), lambda s, lens: (s, 0)),
            ],
            out_specs=pl.BlockSpec((rows, 3 * width), lambda s, lens: (s, 0)),
        ),
        out_shape=jax.ShapeDtypeStruct((seqs * rows, 3 * width), bf16),
        compiler_params=pltpu.CompilerParams(vmem_limit_bytes=VMEM_BYTES),
        cost_estimate=pl.CostEstimate(
            flops=10 * work * HD, bytes_accessed=14 * seqs * rows * width, transcendentals=work
        ),
    )(lengths, qkv, lse, grads)


def swap(values):
    return lax.ppermute(values, "tensor", [(0, 1), (1, 0)])


def across(values, size, bit):
    return lax.ppermute(values, "replica", [(i, i ^ (1 << bit)) for i in range(size)])


def sum_small(values, size):
    for bit in range(size.bit_length() - 1):
        values = values + across(values, size, bit)
    return values


def bit_orders(size):
    bits = list(range(size.bit_length() - 1))
    if len(bits) < 3:
        return [bits] * 3
    return [bits, bits[1:] + bits[:1], [bits[2], bits[0], bits[1]] + bits[3:]]


def sum_chunks(chunks, size):
    me = lax.axis_index("replica")
    orders = bit_orders(size)
    held = list(chunks)
    steps = len(orders[0])
    for step in range(steps):
        for c, order in enumerate(orders):
            bit = order[step]
            mine = (me >> bit) & 1
            half = held[c].shape[0] // 2
            kept = lax.dynamic_slice_in_dim(held[c], mine * half, half, 0)
            sent = lax.dynamic_slice_in_dim(held[c], (1 - mine) * half, half, 0)
            held[c] = kept + across(sent, size, bit)
    for step in reversed(range(steps)):
        for c, order in enumerate(orders):
            bit = order[step]
            mine = (me >> bit) & 1
            other = across(held[c], size, bit)
            first = jnp.where(mine == 0, held[c], other)
            second = jnp.where(mine == 0, other, held[c])
            held[c] = jnp.concatenate((first, second), axis=0)
    return held


def normed(values):
    centered = values - jnp.mean(values, axis=-1, keepdims=True)
    factor = lax.rsqrt(jnp.mean(centered * centered, axis=-1, keepdims=True) + norm_eps)
    return centered * factor, factor


def norm_back(grads, gain, unit, factor):
    scaled = grads * gain
    return factor * (
        scaled
        - jnp.mean(scaled, axis=-1, keepdims=True)
        - unit * jnp.mean(scaled * unit, axis=-1, keepdims=True)
    )


def gelu_both(values):
    cdf = 0.5 * (1.0 + lax.erf(values * (0.5**0.5)))
    density = jnp.exp(-0.5 * values * values) * 0.3989422804014327
    return (values * cdf).astype(bf16), cdf + values * density


def shards(
    size,
    tokens,
    lengths,
    w_qkv,
    qv_bias,
    w_out,
    out_bias,
    ln1_gain,
    ln1_bias,
    w_in,
    in_bias,
    w_down,
    down_bias,
    ln2_gain,
    ln2_bias,
    cotangent,
):
    half = cotangent.shape[0]
    half_seqs = lengths.shape[0] // 2
    depth, width = w_out.shape[1], w_out.shape[0]
    inner_width = w_in.shape[1]
    me = lax.axis_index("tensor")
    pick = lax.dynamic_slice_in_dim
    x_own, x_far = pick(tokens, me * half, half, 0), pick(tokens, (1 - me) * half, half, 0)
    len_own = pick(lengths, me * half_seqs, half_seqs, 0)
    len_far = pick(lengths, (1 - me) * half_seqs, half_seqs, 0)
    w_all = jnp.concatenate((w_qkv[0], w_qkv[1], w_qkv[2]), axis=1)
    bias_pair = qv_bias.astype(f32)
    bias_all = jnp.concatenate((bias_pair[0], jnp.zeros((width,), f32), bias_pair[1]))

    qkv_far = (dot_of(x_far, w_all, 1, 0) + bias_all).astype(bf16)
    att_far, lse_far = attend(len_far, qkv_far)
    out_far = swap(dot_of(att_far, w_out, 1, 0).astype(bf16))
    qkv_own = (dot_of(x_own, w_all, 1, 0) + bias_all).astype(bf16)
    att_own, lse_own = attend(len_own, qkv_own)
    out_own = dot_of(att_own, w_out, 1, 0)
    gain1, gain2 = ln1_gain.astype(f32), ln2_gain.astype(f32)
    unit1, factor1 = normed(
        x_own.astype(f32) + (out_own + out_far.astype(f32) + out_bias.astype(f32))
    )
    hidden = unit1 * gain1 + ln1_bias.astype(f32)
    h_own = hidden.astype(bf16)
    h_far = swap(h_own)

    bias_in = in_bias.astype(f32)
    act_own, slope_own = lax.optimization_barrier(gelu_both(dot_of(h_own, w_in, 1, 0) + bias_in))
    act_far, slope_far = lax.optimization_barrier(gelu_both(dot_of(h_far, w_in, 1, 0) + bias_in))
    down_far = swap(dot_of(act_far, w_down, 1, 0).astype(bf16))
    down_own = dot_of(act_own, w_down, 1, 0)
    unit2, factor2 = normed(
        hidden + (down_own + down_far.astype(f32) + down_bias.astype(f32))
    )
    mixed_out = (unit2 * gain2 + ln2_bias.astype(f32)).astype(bf16)

    cot = cotangent.astype(f32)
    grad_gain2, grad_bias2 = jnp.sum(cot * unit2, axis=0), jnp.sum(cot, axis=0)
    grad_mid = norm_back(cot, gain2, unit2, factor2)
    grad_down_bias = jnp.sum(grad_mid, axis=0)
    gm_own = grad_mid.astype(bf16)
    gm_far = swap(gm_own)
    inner_own = dot_of(gm_own, w_down, 1, 1) * slope_own
    inner_far = dot_of(gm_far, w_down, 1, 1) * slope_far
    grad_in_bias = jnp.sum(inner_own, axis=0) + jnp.sum(inner_far, axis=0)
    gi_own, gi_far = inner_own.astype(bf16), inner_far.astype(bf16)
    gh_far = swap(dot_of(gi_far, w_in, 1, 1).astype(bf16))
    gh_own = dot_of(gi_own, w_in, 1, 1)
    g_down = (dot_of(act_own, gm_own, 0, 0) + dot_of(act_far, gm_far, 0, 0)).astype(bf16)
    g_in = (dot_of(h_own, gi_own, 0, 0) + dot_of(h_far, gi_far, 0, 0)).astype(bf16)

    grad_hidden = grad_mid + (gh_own + gh_far.astype(f32))
    grad_gain1, grad_bias1 = jnp.sum(grad_hidden * unit1, axis=0), jnp.sum(grad_hidden, axis=0)
    grad_first = norm_back(grad_hidden, gain1, unit1, factor1)
    grad_out_bias = jnp.sum(grad_first, axis=0)
    ga_own = grad_first.astype(bf16)
    ga_far = swap(ga_own)
    g_out = (dot_of(att_own, ga_own, 0, 0) + dot_of(att_far, ga_far, 0, 0)).astype(bf16)

    small = sum_small(
        jnp.concatenate(
            (grad_out_bias, grad_gain1, grad_bias1, grad_down_bias, grad_gain2, grad_bias2, grad_in_bias)
        ),
        size,
    )
    rows_down, rows_in, rows_out = inner_width // 3, depth // 3, width // 3
    side = inner_width // 2
    chunks = [
        jnp.concatenate(
            (
                g_down[c * rows_down : (c + 1) * rows_down],
                g_in[c * rows_in : (c + 1) * rows_in, :side],
                g_in[c * rows_in : (c + 1) * rows_in, side:],
                g_out[c * rows_out : (c + 1) * rows_out],
            ),
            axis=0,
        )
        for c in range(3)
    ]
    early = sum_chunks(chunks, size)

    gatt_own = dot_of(ga_own, w_out, 1, 1).astype(bf16)
    gatt_far = dot_of(ga_far, w_out, 1, 1).astype(bf16)
    dq_own = attend_back(len_own, qkv_own, lse_own, gatt_own)
    dq_far = attend_back(len_far, qkv_far, lse_far, gatt_far)
    g_qkv = (dot_of(x_own, dq_own, 0, 0) + dot_of(x_far, dq_far, 0, 0)).astype(bf16)
    late = sum_chunks([g_qkv[:, c * width : (c + 1) * width] for c in range(3)], size)
    sums = jnp.sum(dq_own.astype(f32), axis=0) + jnp.sum(dq_far.astype(f32), axis=0)
    sums = sum_small(jnp.concatenate((sums[:width], sums[2 * width :])), size)
    ig_far = swap(dot_of(dq_far, w_all, 1, 1).astype(bf16))
    input_grad = dot_of(dq_own, w_all, 1, 1) + ig_far.astype(f32) + grad_first

    shared = small[: 6 * depth]
    shared = shared + swap(shared)
    shared = [shared[i * depth : (i + 1) * depth] for i in range(6)]
    a, b = rows_down, rows_down + rows_in
    full_down = jnp.concatenate([part[:a] for part in early], axis=0).astype(f32)
    full_in = jnp.concatenate(
        [jnp.concatenate((part[a:b], part[b : b + rows_in]), axis=1) for part in early], axis=0
    ).astype(f32)
    full_out = jnp.concatenate([part[b + rows_in :] for part in early], axis=0).astype(f32)
    full_qkv = jnp.stack(late).astype(f32)
    return (
        mixed_out,
        input_grad,
        full_qkv,
        sums.reshape(2, width),
        full_out,
        shared[0],
        shared[1],
        shared[2],
        full_in,
        small[6 * depth :],
        full_down,
        shared[3],
        shared[4],
        shared[5],
    )


def solution(mesh):
    in_specs = (
        P("replica", None),
        P("replica"),
        P(None, None, "tensor"),
        P(None, "tensor"),
        P("tensor", None),
        P(),
        P(),
        P(),
        P(None, "tensor"),
        P("tensor"),
        P("tensor", None),
        P(),
        P(),
        P(),
        P(("replica", "tensor"), None),
    )
    out_specs = (
        P(("replica", "tensor"), None),
        P(("replica", "tensor"), None),
        P(None, None, "tensor"),
        P(None, "tensor"),
        P("tensor", None),
        P(),
        P(),
        P(),
        P(None, "tensor"),
        P("tensor"),
        P("tensor", None),
        P(),
        P(),
        P(),
    )
    return jax.shard_map(
        functools.partial(shards, mesh.shape["replica"]),
        mesh=mesh,
        in_specs=in_specs,
        out_specs=out_specs,
        check_vma=False,
    )
```

```python
import functools

import jax
import jax.numpy as jnp
from jax import lax
from jax.experimental import pallas as pl
from jax.experimental.pallas import tpu as pltpu
from jax.sharding import PartitionSpec as P

HD = 64
norm_eps = 1e-06
f32 = jnp.float32
bf16 = jnp.bfloat16
VMEM_BYTES = 48 * 1024 * 1024


def dot_of(left, right, left_dim, right_dim):
    return lax.dot_general(
        left, right, (((left_dim,), (right_dim,)), ((), ())), preferred_element_type=f32
    )


def scores_of(keys, queries, length):
    scores = dot_of(keys, queries, 1, 1)
    places = lax.broadcasted_iota(jnp.int32, scores.shape, 0)
    return jnp.where(places < length, scores, -1000000000.0)


def forward_kernel(width, lengths_ref, qkv_ref, out_ref, lse_ref):
    length = lengths_ref[pl.program_id(0)]
    pair = 2 * HD
    for start in range(0, width, pair):
        both = []
        for head in range(start // HD, start // HD + 2):
            at = head * HD
            queries = qkv_ref[:, at : at + HD] * jnp.asarray(HD**-0.5, bf16)
            keys = qkv_ref[:, width + at : width + at + HD]
            values = qkv_ref[:, 2 * width + at : 2 * width + at + HD]
            scores = scores_of(keys, queries, length)
            top = jnp.max(scores, axis=0, keepdims=True)
            weights = jnp.exp(scores - top)
            total = jnp.sum(weights, axis=0, keepdims=True)
            probs = (weights * (1.0 / total)).astype(bf16)
            lse_ref[0, head : head + 1, :] = top + jnp.log(total)
            both.append(dot_of(values, probs, 0, 0))
        out_ref[:, start : start + pair] = jnp.concatenate(both, axis=0).T.astype(bf16)


def backward_kernel(width, lengths_ref, qkv_ref, lse_ref, grad_ref, out_ref):
    length = lengths_ref[pl.program_id(0)]
    pair = 2 * HD
    factor = HD**-0.5
    for start in range(0, width, pair):
        grad_q, grad_k, grad_v = [], [], []
        for head in range(start // HD, start // HD + 2):
            at = head * HD
            queries = qkv_ref[:, at : at + HD] * jnp.asarray(factor, bf16)
            keys = qkv_ref[:, width + at : width + at + HD]
            values = qkv_ref[:, 2 * width + at : 2 * width + at + HD]
            grads = grad_ref[:, at : at + HD]
            scores = scores_of(keys, queries, length)
            probs = jnp.exp(scores - lse_ref[0, head : head + 1, :])
            grad_probs = dot_of(values, grads, 1, 1)
            delta = jnp.sum(grad_probs * probs, axis=0, keepdims=True)
            grad_scores = (probs * (grad_probs - delta)).astype(bf16)
            grad_q.append(dot_of(keys, grad_scores, 0, 0) * factor)
            grad_k.append(dot_of(grad_scores, queries, 1, 0))
            grad_v.append(dot_of(probs.astype(bf16), grads, 1, 0))
        out_ref[:, start : start + pair] = jnp.concatenate(grad_q, axis=0).T.astype(bf16)
        at = width + start
        out_ref[:, at : at + pair] = jnp.concatenate(grad_k, axis=1).astype(bf16)
        at = 2 * width + start
        out_ref[:, at : at + pair] = jnp.concatenate(grad_v, axis=1).astype(bf16)


def attend(lengths, qkv):
    seqs = lengths.shape[0]
    rows, width = qkv.shape[0] // seqs, qkv.shape[1] // 3
    heads = width // HD
    work = seqs * heads * rows * rows
    return pl.pallas_call(
        functools.partial(forward_kernel, width),
        grid_spec=pltpu.PrefetchScalarGridSpec(
            num_scalar_prefetch=1,
            grid=(seqs,),
            in_specs=[pl.BlockSpec((rows, 3 * width), lambda s, lens: (s, 0))],
            out_specs=[
                pl.BlockSpec((rows, width), lambda s, lens: (s, 0)),
                pl.BlockSpec((1, heads, rows), lambda s, lens: (s, 0, 0)),
            ],
        ),
        out_shape=[
            jax.ShapeDtypeStruct((seqs * rows, width), bf16),
            jax.ShapeDtypeStruct((seqs, heads, rows), f32),
        ],
        compiler_params=pltpu.CompilerParams(vmem_limit_bytes=VMEM_BYTES),
        cost_estimate=pl.CostEstimate(
            flops=4 * work * HD, bytes_accessed=8 * seqs * rows * width, transcendentals=work
        ),
    )(lengths, qkv)


def attend_back(lengths, qkv, lse, grads):
    seqs = lengths.shape[0]
    rows, width = qkv.shape[0] // seqs, qkv.shape[1] // 3
    heads = width // HD
    work = seqs * heads * rows * rows
    return pl.pallas_call(
        functools.partial(backward_kernel, width),
        grid_spec=pltpu.PrefetchScalarGridSpec(
            num_scalar_prefetch=1,
            grid=(seqs,),
            in_specs=[
                pl.BlockSpec((rows, 3 * width), lambda s, lens: (s, 0)),
                pl.BlockSpec((1, heads, rows), lambda s, lens: (s, 0, 0)),
                pl.BlockSpec((rows, width), lambda s, lens: (s, 0)),
            ],
            out_specs=pl.BlockSpec((rows, 3 * width), lambda s, lens: (s, 0)),
        ),
        out_shape=jax.ShapeDtypeStruct((seqs * rows, 3 * width), bf16),
        compiler_params=pltpu.CompilerParams(vmem_limit_bytes=VMEM_BYTES),
        cost_estimate=pl.CostEstimate(
            flops=10 * work * HD, bytes_accessed=14 * seqs * rows * width, transcendentals=work
        ),
    )(lengths, qkv, lse, grads)


def swap(values):
    return lax.ppermute(values, "tensor", [(0, 1), (1, 0)])


def across(values, size, bit):
    return lax.ppermute(values, "replica", [(i, i ^ (1 << bit)) for i in range(size)])


def sum_small(values, size):
    for bit in range(size.bit_length() - 1):
        values = values + across(values, size, bit)
    return values


def bit_orders(size):
    bits = list(range(size.bit_length() - 1))
    if len(bits) < 3:
        return [bits] * 3
    return [bits, bits[1:] + bits[:1], [bits[2], bits[0], bits[1]] + bits[3:]]


def sum_chunks(chunks, size):
    me = lax.axis_index("replica")
    orders = bit_orders(size)
    held = list(chunks)
    steps = len(orders[0])
    for step in range(steps):
        for c, order in enumerate(orders):
            bit = order[step]
            mine = (me >> bit) & 1
            half = held[c].shape[0] // 2
            kept = lax.dynamic_slice_in_dim(held[c], mine * half, half, 0)
            sent = lax.dynamic_slice_in_dim(held[c], (1 - mine) * half, half, 0)
            held[c] = kept + across(sent, size, bit)
    for step in reversed(range(steps)):
        for c, order in enumerate(orders):
            bit = order[step]
            mine = (me >> bit) & 1
            other = across(held[c], size, bit)
            first = jnp.where(mine == 0, held[c], other)
            second = jnp.where(mine == 0, other, held[c])
            held[c] = jnp.concatenate((first, second), axis=0)
    return held


def bits_of(size):
    return size.bit_length() - 1


def sum_kernel(size, orders, in_ref, out_ref, acc, landed, send_sem, recv_sem):
    me = lax.axis_index("replica")
    steps = bits_of(size)
    full = in_ref.shape[1]
    barrier = pltpu.get_barrier_semaphore()
    for bit in range(steps):
        pl.semaphore_signal(
            barrier,
            inc=1,
            device_id={"replica": me ^ (1 << bit)},
            device_id_type=pl.DeviceIdType.MESH,
        )
    pl.semaphore_wait(barrier, steps)

    def copy_of(source, target, c, step, bit):
        return pltpu.make_async_remote_copy(
            src_ref=source,
            dst_ref=target,
            send_sem=send_sem.at[c, step],
            recv_sem=recv_sem.at[c, step],
            device_id={"replica": me ^ (1 << bit)},
            device_id_type=pl.DeviceIdType.MESH,
        )

    base = [0] * len(orders)
    flying = [None] * len(orders)
    for step in range(steps + 1):
        for c, order in enumerate(orders):
            if step > 0:
                half = full >> step
                flying[c].wait()
                held = in_ref if step == 1 else acc
                into = out_ref if step == steps else acc
                start = full - 2 * half
                block = 64

                @pl.loop(0, half // block)
                def _(i, c=c, held=held, into=into, start=start, place=base[c]):
                    rows = pl.ds(pl.multiple_of(place + i * block, block), block)
                    came = pl.ds(pl.multiple_of(start + i * block, block), block)
                    total = held[c, rows, :].astype(f32) + landed[c, came, :].astype(f32)
                    into[c, rows, :] = total.astype(bf16)

            if step < steps:
                bit = order[step]
                half = full >> (step + 1)
                mine = (me >> bit) & 1
                away = pl.ds(pl.multiple_of(base[c] + (1 - mine) * half, half), half)
                base[c] = base[c] + mine * half
                held = in_ref if step == 0 else acc
                flying[c] = copy_of(
                    held.at[c, away], landed.at[c, pl.ds(full - 2 * half, half)], c, step, bit
                )
                flying[c].start()
    for step in range(steps):
        for c, order in enumerate(orders):
            bit = order[steps - 1 - step]
            held = full >> (steps - step)
            if step > 0:
                flying[c].wait()
            rows = out_ref.at[c, pl.ds(pl.multiple_of(base[c], held), held)]
            flying[c] = copy_of(rows, rows, c, steps + step, bit)
            flying[c].start()
            base[c] = base[c] - ((me >> bit) & 1) * held
    for c in range(len(orders)):
        flying[c].wait()


def sum_packed(packed, size):
    rows = packed.shape[1]
    if size & (size - 1) or size < 8 or rows % (64 * size):
        return jnp.stack(sum_chunks([packed[c] for c in range(packed.shape[0])], size))
    return pl.pallas_call(
        functools.partial(sum_kernel, size, bit_orders(size)),
        out_shape=jax.ShapeDtypeStruct(packed.shape, bf16),
        in_specs=[pl.BlockSpec(memory_space=pltpu.VMEM)],
        out_specs=pl.BlockSpec(memory_space=pltpu.VMEM),
        scratch_shapes=[
            pltpu.VMEM(packed.shape, bf16),
            pltpu.VMEM(packed.shape, bf16),
            pltpu.SemaphoreType.DMA((3, 2 * bits_of(size))),
            pltpu.SemaphoreType.DMA((3, 2 * bits_of(size))),
        ],
        compiler_params=pltpu.CompilerParams(
            collective_id=0, has_side_effects=True, vmem_limit_bytes=VMEM_BYTES
        ),
    )(packed)


def pieces_of(*refs):
    side = refs[-1].shape[-1]
    top = 0
    for ref in refs[:-1]:
        for left in range(0, ref.shape[1], side):
            yield ref, slice(left, left + side), slice(top, top + ref.shape[0])
            top += ref.shape[0]


def pack_kernel(*refs):
    for ref, columns, rows in pieces_of(*refs):
        refs[-1][0, rows, :] = ref[:, columns].astype(bf16)


def unpack_kernel(packed_ref, down_ref, in_ref, out_ref, qkv_ref):
    last = 0
    for ref, columns, rows in pieces_of(down_ref, in_ref, out_ref, packed_ref):
        ref[:, columns] = packed_ref[0, rows, :].astype(f32)
        last = rows.stop
    qkv_ref[0] = packed_ref[0, last:, :].astype(f32)


def pack(g_down, g_in, g_out, g_qkv):
    width = g_out.shape[0]
    depth = g_out.shape[1]
    cut = lambda a: pl.BlockSpec((a.shape[0] // 3, a.shape[1]), lambda c: (c, 0))
    rows = (g_down.size + g_in.size + g_out.size + g_qkv.size) // (3 * width)
    return pl.pallas_call(
        pack_kernel,
        grid=(3,),
        in_specs=[cut(g_down), cut(g_in), cut(g_out), pl.BlockSpec((depth, width), lambda c: (0, c))],
        out_specs=pl.BlockSpec((1, rows, width), lambda c: (c, 0, 0)),
        out_shape=jax.ShapeDtypeStruct((3, rows, width), bf16),
        compiler_params=pltpu.CompilerParams(vmem_limit_bytes=VMEM_BYTES),
    )(g_down, g_in, g_out, g_qkv)


def unpack(packed, shapes, qkv_shape):
    return pl.pallas_call(
        unpack_kernel,
        grid=(3,),
        in_specs=[pl.BlockSpec((1,) + packed.shape[1:], lambda c: (c, 0, 0))],
        out_specs=[pl.BlockSpec((a[0] // 3, a[1]), lambda c: (c, 0)) for a in shapes]
        + [pl.BlockSpec((1,) + qkv_shape[1:], lambda c: (c, 0, 0))],
        out_shape=[jax.ShapeDtypeStruct(a, f32) for a in shapes]
        + [jax.ShapeDtypeStruct(qkv_shape, f32)],
        compiler_params=pltpu.CompilerParams(vmem_limit_bytes=VMEM_BYTES),
    )(packed)


def normed(values):
    centered = values - jnp.mean(values, axis=-1, keepdims=True)
    factor = lax.rsqrt(jnp.mean(centered * centered, axis=-1, keepdims=True) + norm_eps)
    return centered * factor, factor


def norm_back(grads, gain, unit, factor):
    scaled = grads * gain
    return factor * (
        scaled
        - jnp.mean(scaled, axis=-1, keepdims=True)
        - unit * jnp.mean(scaled * unit, axis=-1, keepdims=True)
    )


def gelu_both(values):
    cdf = 0.5 * (1.0 + lax.erf(values * (0.5**0.5)))
    density = jnp.exp(-0.5 * values * values) * 0.3989422804014327
    return (values * cdf).astype(bf16), cdf + values * density


def shards(
    size,
    tokens,
    lengths,
    w_qkv,
    qv_bias,
    w_out,
    out_bias,
    ln1_gain,
    ln1_bias,
    w_in,
    in_bias,
    w_down,
    down_bias,
    ln2_gain,
    ln2_bias,
    cotangent,
):
    half = cotangent.shape[0]
    half_seqs = lengths.shape[0] // 2
    depth, width = w_out.shape[1], w_out.shape[0]
    me = lax.axis_index("tensor")
    pick = lax.dynamic_slice_in_dim
    x_own, x_far = pick(tokens, me * half, half, 0), pick(tokens, (1 - me) * half, half, 0)
    len_own = pick(lengths, me * half_seqs, half_seqs, 0)
    len_far = pick(lengths, (1 - me) * half_seqs, half_seqs, 0)
    w_all = jnp.concatenate((w_qkv[0], w_qkv[1], w_qkv[2]), axis=1)
    bias_pair = qv_bias.astype(f32)
    bias_all = jnp.concatenate((bias_pair[0], jnp.zeros((width,), f32), bias_pair[1]))

    qkv_far = (dot_of(x_far, w_all, 1, 0) + bias_all).astype(bf16)
    att_far, lse_far = attend(len_far, qkv_far)
    out_far = swap(dot_of(att_far, w_out, 1, 0).astype(bf16))
    qkv_own = (dot_of(x_own, w_all, 1, 0) + bias_all).astype(bf16)
    att_own, lse_own = attend(len_own, qkv_own)
    out_own = dot_of(att_own, w_out, 1, 0)
    gain1, gain2 = ln1_gain.astype(f32), ln2_gain.astype(f32)
    unit1, factor1 = normed(
        x_own.astype(f32) + (out_own + out_far.astype(f32) + out_bias.astype(f32))
    )
    hidden = unit1 * gain1 + ln1_bias.astype(f32)
    h_own = hidden.astype(bf16)
    h_far = swap(h_own)

    bias_in = in_bias.astype(f32)
    act_own, slope_own = lax.optimization_barrier(gelu_both(dot_of(h_own, w_in, 1, 0) + bias_in))
    act_far, slope_far = lax.optimization_barrier(gelu_both(dot_of(h_far, w_in, 1, 0) + bias_in))
    down_far = swap(dot_of(act_far, w_down, 1, 0).astype(bf16))
    down_own = dot_of(act_own, w_down, 1, 0)
    unit2, factor2 = normed(
        hidden + (down_own + down_far.astype(f32) + down_bias.astype(f32))
    )
    mixed_out = (unit2 * gain2 + ln2_bias.astype(f32)).astype(bf16)

    cot = cotangent.astype(f32)
    grad_gain2, grad_bias2 = jnp.sum(cot * unit2, axis=0), jnp.sum(cot, axis=0)
    grad_mid = norm_back(cot, gain2, unit2, factor2)
    grad_down_bias = jnp.sum(grad_mid, axis=0)
    gm_own = grad_mid.astype(bf16)
    gm_far = swap(gm_own)
    inner_own = dot_of(gm_own, w_down, 1, 1) * slope_own
    inner_far = dot_of(gm_far, w_down, 1, 1) * slope_far
    grad_in_bias = jnp.sum(inner_own, axis=0) + jnp.sum(inner_far, axis=0)
    gi_own, gi_far = inner_own.astype(bf16), inner_far.astype(bf16)
    gh_far = swap(dot_of(gi_far, w_in, 1, 1).astype(bf16))
    gh_own = dot_of(gi_own, w_in, 1, 1)
    g_down = (dot_of(act_own, gm_own, 0, 0) + dot_of(act_far, gm_far, 0, 0)).astype(bf16)
    g_in = (dot_of(h_own, gi_own, 0, 0) + dot_of(h_far, gi_far, 0, 0)).astype(bf16)

    grad_hidden = grad_mid + (gh_own + gh_far.astype(f32))
    grad_gain1, grad_bias1 = jnp.sum(grad_hidden * unit1, axis=0), jnp.sum(grad_hidden, axis=0)
    grad_first = norm_back(grad_hidden, gain1, unit1, factor1)
    grad_out_bias = jnp.sum(grad_first, axis=0)
    ga_own = grad_first.astype(bf16)
    ga_far = swap(ga_own)
    g_out = (dot_of(att_own, ga_own, 0, 0) + dot_of(att_far, ga_far, 0, 0)).astype(bf16)

    small = sum_small(
        jnp.concatenate(
            (grad_out_bias, grad_gain1, grad_bias1, grad_down_bias, grad_gain2, grad_bias2, grad_in_bias)
        ),
        size,
    )
    gatt_own = dot_of(ga_own, w_out, 1, 1).astype(bf16)
    gatt_far = dot_of(ga_far, w_out, 1, 1).astype(bf16)
    dq_own = attend_back(len_own, qkv_own, lse_own, gatt_own)
    dq_far = attend_back(len_far, qkv_far, lse_far, gatt_far)
    g_qkv = (dot_of(x_own, dq_own, 0, 0) + dot_of(x_far, dq_far, 0, 0)).astype(bf16)
    sums = jnp.sum(dq_own.astype(f32), axis=0) + jnp.sum(dq_far.astype(f32), axis=0)
    sums = sum_small(jnp.concatenate((sums[:width], sums[2 * width :])), size)
    ig_far = swap(dot_of(dq_far, w_all, 1, 1).astype(bf16))
    input_grad = dot_of(dq_own, w_all, 1, 1) + ig_far.astype(f32) + grad_first

    shared = small[: 6 * depth]
    shared = shared + swap(shared)
    shared = [shared[i * depth : (i + 1) * depth] for i in range(6)]
    g_down, g_in, g_out, g_qkv, sums, shared, small, input_grad = lax.optimization_barrier(
        (g_down, g_in, g_out, g_qkv, sums, shared, small, input_grad)
    )
    full_down, full_in, full_out, full_qkv = unpack(
        sum_packed(pack(g_down, g_in, g_out, g_qkv), size),
        (g_down.shape, g_in.shape, g_out.shape),
        w_qkv.shape,
    )
    return (
        mixed_out,
        input_grad,
        full_qkv,
        sums.reshape(2, width),
        full_out,
        shared[0],
        shared[1],
        shared[2],
        full_in,
        small[6 * depth :],
        full_down,
        shared[3],
        shared[4],
        shared[5],
    )


def solution(mesh):
    in_specs = (
        P("replica", None),
        P("replica"),
        P(None, None, "tensor"),
        P(None, "tensor"),
        P("tensor", None),
        P(),
        P(),
        P(),
        P(None, "tensor"),
        P("tensor"),
        P("tensor", None),
        P(),
        P(),
        P(),
        P(("replica", "tensor"), None),
    )
    out_specs = (
        P(("replica", "tensor"), None),
        P(("replica", "tensor"), None),
        P(None, None, "tensor"),
        P(None, "tensor"),
        P("tensor", None),
        P(),
        P(),
        P(),
        P(None, "tensor"),
        P("tensor"),
        P("tensor", None),
        P(),
        P(),
        P(),
    )
    return jax.shard_map(
        functools.partial(shards, mesh.shape["replica"]),
        mesh=mesh,
        in_specs=in_specs,
        out_specs=out_specs,
        check_vma=False,
    )
```

```python
import functools

import jax
import jax.numpy as jnp
from jax import lax
from jax.experimental import pallas as pl
from jax.experimental.pallas import tpu as pltpu
from jax.sharding import PartitionSpec as P

HD = 64
norm_eps = 1e-06
f32 = jnp.float32
bf16 = jnp.bfloat16
VMEM_BYTES = 48 * 1024 * 1024


def dot_of(left, right, left_dim, right_dim):
    return lax.dot_general(
        left, right, (((left_dim,), (right_dim,)), ((), ())), preferred_element_type=f32
    )


def scores_of(keys, queries, length):
    scores = dot_of(keys, queries, 1, 1)
    places = lax.broadcasted_iota(jnp.int32, scores.shape, 0)
    return jnp.where(places < length, scores, -1000000000.0)


def forward_kernel(width, lengths_ref, qkv_ref, out_ref, lse_ref):
    length = lengths_ref[pl.program_id(0)]
    pair = 2 * HD
    for start in range(0, width, pair):
        both = []
        for head in range(start // HD, start // HD + 2):
            at = head * HD
            queries = qkv_ref[:, at : at + HD] * jnp.asarray(HD**-0.5, bf16)
            keys = qkv_ref[:, width + at : width + at + HD]
            values = qkv_ref[:, 2 * width + at : 2 * width + at + HD]
            scores = scores_of(keys, queries, length)
            top = jnp.max(scores, axis=0, keepdims=True)
            weights = jnp.exp(scores - top)
            total = jnp.sum(weights, axis=0, keepdims=True)
            probs = (weights * (1.0 / total)).astype(bf16)
            lse_ref[0, head : head + 1, :] = top + jnp.log(total)
            both.append(dot_of(values, probs, 0, 0))
        out_ref[:, start : start + pair] = jnp.concatenate(both, axis=0).T.astype(bf16)


def backward_kernel(width, lengths_ref, qkv_ref, lse_ref, grad_ref, out_ref):
    length = lengths_ref[pl.program_id(0)]
    pair = 2 * HD
    factor = HD**-0.5
    for start in range(0, width, pair):
        grad_q, grad_k, grad_v = [], [], []
        for head in range(start // HD, start // HD + 2):
            at = head * HD
            queries = qkv_ref[:, at : at + HD] * jnp.asarray(factor, bf16)
            keys = qkv_ref[:, width + at : width + at + HD]
            values = qkv_ref[:, 2 * width + at : 2 * width + at + HD]
            grads = grad_ref[:, at : at + HD]
            scores = scores_of(keys, queries, length)
            probs = jnp.exp(scores - lse_ref[0, head : head + 1, :])
            grad_probs = dot_of(values, grads, 1, 1)
            delta = jnp.sum(grad_probs * probs, axis=0, keepdims=True)
            grad_scores = (probs * (grad_probs - delta)).astype(bf16)
            grad_q.append(dot_of(keys, grad_scores, 0, 0) * factor)
            grad_k.append(dot_of(grad_scores, queries, 1, 0))
            grad_v.append(dot_of(probs.astype(bf16), grads, 1, 0))
        out_ref[:, start : start + pair] = jnp.concatenate(grad_q, axis=0).T.astype(bf16)
        at = width + start
        out_ref[:, at : at + pair] = jnp.concatenate(grad_k, axis=1).astype(bf16)
        at = 2 * width + start
        out_ref[:, at : at + pair] = jnp.concatenate(grad_v, axis=1).astype(bf16)


def attend(lengths, qkv):
    seqs = lengths.shape[0]
    rows, width = qkv.shape[0] // seqs, qkv.shape[1] // 3
    heads = width // HD
    work = seqs * heads * rows * rows
    return pl.pallas_call(
        functools.partial(forward_kernel, width),
        grid_spec=pltpu.PrefetchScalarGridSpec(
            num_scalar_prefetch=1,
            grid=(seqs,),
            in_specs=[pl.BlockSpec((rows, 3 * width), lambda s, lens: (s, 0))],
            out_specs=[
                pl.BlockSpec((rows, width), lambda s, lens: (s, 0)),
                pl.BlockSpec((1, heads, rows), lambda s, lens: (s, 0, 0)),
            ],
        ),
        out_shape=[
            jax.ShapeDtypeStruct((seqs * rows, width), bf16),
            jax.ShapeDtypeStruct((seqs, heads, rows), f32),
        ],
        compiler_params=pltpu.CompilerParams(vmem_limit_bytes=VMEM_BYTES),
        cost_estimate=pl.CostEstimate(
            flops=4 * work * HD, bytes_accessed=8 * seqs * rows * width, transcendentals=work
        ),
    )(lengths, qkv)


def attend_back(lengths, qkv, lse, grads):
    seqs = lengths.shape[0]
    rows, width = qkv.shape[0] // seqs, qkv.shape[1] // 3
    heads = width // HD
    work = seqs * heads * rows * rows
    return pl.pallas_call(
        functools.partial(backward_kernel, width),
        grid_spec=pltpu.PrefetchScalarGridSpec(
            num_scalar_prefetch=1,
            grid=(seqs,),
            in_specs=[
                pl.BlockSpec((rows, 3 * width), lambda s, lens: (s, 0)),
                pl.BlockSpec((1, heads, rows), lambda s, lens: (s, 0, 0)),
                pl.BlockSpec((rows, width), lambda s, lens: (s, 0)),
            ],
            out_specs=pl.BlockSpec((rows, 3 * width), lambda s, lens: (s, 0)),
        ),
        out_shape=jax.ShapeDtypeStruct((seqs * rows, 3 * width), bf16),
        compiler_params=pltpu.CompilerParams(vmem_limit_bytes=VMEM_BYTES),
        cost_estimate=pl.CostEstimate(
            flops=10 * work * HD, bytes_accessed=14 * seqs * rows * width, transcendentals=work
        ),
    )(lengths, qkv, lse, grads)


def swap(values):
    return lax.ppermute(values, "tensor", [(0, 1), (1, 0)])


def across(values, size, bit):
    return lax.ppermute(values, "replica", [(i, i ^ (1 << bit)) for i in range(size)])


def sum_small(values, size):
    for bit in range(size.bit_length() - 1):
        values = values + across(values, size, bit)
    return values


def bit_orders(size):
    bits = list(range(size.bit_length() - 1))
    if len(bits) < 3:
        return [bits] * 3
    return [bits, bits[1:] + bits[:1], [bits[2], bits[0], bits[1]] + bits[3:]]


def sum_chunks(chunks, size):
    me = lax.axis_index("replica")
    orders = bit_orders(size)
    held = list(chunks)
    steps = len(orders[0])
    for step in range(steps):
        for c, order in enumerate(orders):
            bit = order[step]
            mine = (me >> bit) & 1
            half = held[c].shape[0] // 2
            kept = lax.dynamic_slice_in_dim(held[c], mine * half, half, 0)
            sent = lax.dynamic_slice_in_dim(held[c], (1 - mine) * half, half, 0)
            held[c] = kept + across(sent, size, bit)
    for step in reversed(range(steps)):
        for c, order in enumerate(orders):
            bit = order[step]
            mine = (me >> bit) & 1
            other = across(held[c], size, bit)
            first = jnp.where(mine == 0, held[c], other)
            second = jnp.where(mine == 0, other, held[c])
            held[c] = jnp.concatenate((first, second), axis=0)
    return held


def bits_of(size):
    return size.bit_length() - 1


def sum_kernel(size, orders, in_ref, out_ref, acc, landed, send_sem, recv_sem):
    me = lax.axis_index("replica")
    steps = bits_of(size)
    full = in_ref.shape[1]
    barrier = pltpu.get_barrier_semaphore()
    for bit in range(steps):
        pl.semaphore_signal(
            barrier,
            inc=1,
            device_id={"replica": me ^ (1 << bit)},
            device_id_type=pl.DeviceIdType.MESH,
        )
    pl.semaphore_wait(barrier, steps)

    def copy_of(source, target, c, step, bit):
        return pltpu.make_async_remote_copy(
            src_ref=source,
            dst_ref=target,
            send_sem=send_sem.at[c, step],
            recv_sem=recv_sem.at[c, step],
            device_id={"replica": me ^ (1 << bit)},
            device_id_type=pl.DeviceIdType.MESH,
        )

    turns = [*range(0, len(orders), 2), *range(1, len(orders), 2)]
    base = [0] * len(orders)
    flying = [None] * len(orders)
    for step in range(steps + 1):
        for c in turns:
            order = orders[c]
            if step > 0:
                half = full >> step
                flying[c].wait()
                held = in_ref if step == 1 else acc
                into = out_ref if step == steps else acc
                start = full - 2 * half
                block = 32

                @pl.loop(0, half // block)
                def _(i, c=c, held=held, into=into, start=start, place=base[c]):
                    rows = pl.ds(pl.multiple_of(place + i * block, block), block)
                    came = pl.ds(pl.multiple_of(start + i * block, block), block)
                    total = held[c, rows, :].astype(f32) + landed[c, came, :].astype(f32)
                    into[c, rows, :] = total.astype(bf16)

            if step < steps:
                bit = order[step]
                half = full >> (step + 1)
                mine = (me >> bit) & 1
                away = pl.ds(pl.multiple_of(base[c] + (1 - mine) * half, half), half)
                base[c] = base[c] + mine * half
                held = in_ref if step == 0 else acc
                flying[c] = copy_of(
                    held.at[c, away], landed.at[c, pl.ds(full - 2 * half, half)], c, step, bit
                )
                flying[c].start()
    for step in range(steps):
        for c in turns:
            bit = orders[c][steps - 1 - step]
            held = full >> (steps - step)
            if step > 0:
                flying[c].wait()
            rows = out_ref.at[c, pl.ds(pl.multiple_of(base[c], held), held)]
            flying[c] = copy_of(rows, rows, c, steps + step, bit)
            flying[c].start()
            base[c] = base[c] - ((me >> bit) & 1) * held
    for c in turns:
        flying[c].wait()


def sum_packed(packed, size):
    rows = packed.shape[1]
    if size & (size - 1) or size < 8 or rows % (64 * size):
        return jnp.stack(sum_chunks([packed[c] for c in range(packed.shape[0])], size))
    shape = packed.shape
    packed = packed.reshape(2 * shape[0], rows // 2, shape[2])
    orders = [order for order in bit_orders(size) for _ in range(2)]
    return pl.pallas_call(
        functools.partial(sum_kernel, size, orders),
        out_shape=jax.ShapeDtypeStruct(packed.shape, bf16),
        in_specs=[pl.BlockSpec(memory_space=pltpu.VMEM)],
        out_specs=pl.BlockSpec(memory_space=pltpu.VMEM),
        scratch_shapes=[
            pltpu.VMEM(packed.shape, bf16),
            pltpu.VMEM(packed.shape, bf16),
            pltpu.SemaphoreType.DMA((6, 2 * bits_of(size))),
            pltpu.SemaphoreType.DMA((6, 2 * bits_of(size))),
        ],
        compiler_params=pltpu.CompilerParams(
            collective_id=0, has_side_effects=True, vmem_limit_bytes=VMEM_BYTES
        ),
    )(packed).reshape(shape)


def pieces_of(*refs):
    side = refs[-1].shape[-1]
    top = 0
    for ref in refs[:-1]:
        for left in range(0, ref.shape[1], side):
            yield ref, slice(left, left + side), slice(top, top + ref.shape[0])
            top += ref.shape[0]


def pack_kernel(*refs):
    for ref, columns, rows in pieces_of(*refs):
        refs[-1][0, rows, :] = ref[:, columns].astype(bf16)


def unpack_kernel(packed_ref, down_ref, in_ref, out_ref, qkv_ref):
    last = 0
    for ref, columns, rows in pieces_of(down_ref, in_ref, out_ref, packed_ref):
        ref[:, columns] = packed_ref[0, rows, :].astype(f32)
        last = rows.stop
    qkv_ref[0] = packed_ref[0, last:, :].astype(f32)


def pack(g_down, g_in, g_out, g_qkv):
    width = g_out.shape[0]
    depth = g_out.shape[1]
    cut = lambda a: pl.BlockSpec((a.shape[0] // 3, a.shape[1]), lambda c: (c, 0))
    rows = (g_down.size + g_in.size + g_out.size + g_qkv.size) // (3 * width)
    return pl.pallas_call(
        pack_kernel,
        grid=(3,),
        in_specs=[cut(g_down), cut(g_in), cut(g_out), pl.BlockSpec((depth, width), lambda c: (0, c))],
        out_specs=pl.BlockSpec((1, rows, width), lambda c: (c, 0, 0)),
        out_shape=jax.ShapeDtypeStruct((3, rows, width), bf16),
        compiler_params=pltpu.CompilerParams(vmem_limit_bytes=VMEM_BYTES),
    )(g_down, g_in, g_out, g_qkv)


def unpack(packed, shapes, qkv_shape):
    return pl.pallas_call(
        unpack_kernel,
        grid=(3,),
        in_specs=[pl.BlockSpec((1,) + packed.shape[1:], lambda c: (c, 0, 0))],
        out_specs=[pl.BlockSpec((a[0] // 3, a[1]), lambda c: (c, 0)) for a in shapes]
        + [pl.BlockSpec((1,) + qkv_shape[1:], lambda c: (c, 0, 0))],
        out_shape=[jax.ShapeDtypeStruct(a, f32) for a in shapes]
        + [jax.ShapeDtypeStruct(qkv_shape, f32)],
        compiler_params=pltpu.CompilerParams(vmem_limit_bytes=VMEM_BYTES),
    )(packed)


def normed(values):
    centered = values - jnp.mean(values, axis=-1, keepdims=True)
    factor = lax.rsqrt(jnp.mean(centered * centered, axis=-1, keepdims=True) + norm_eps)
    return centered * factor, factor


def norm_back(grads, gain, unit, factor):
    scaled = grads * gain
    return factor * (
        scaled
        - jnp.mean(scaled, axis=-1, keepdims=True)
        - unit * jnp.mean(scaled * unit, axis=-1, keepdims=True)
    )


def gelu_both(values):
    cdf = 0.5 * (1.0 + lax.erf(values * (0.5**0.5)))
    density = jnp.exp(-0.5 * values * values) * 0.3989422804014327
    return (values * cdf).astype(bf16), cdf + values * density


def shards(
    size,
    tokens,
    lengths,
    w_qkv,
    qv_bias,
    w_out,
    out_bias,
    ln1_gain,
    ln1_bias,
    w_in,
    in_bias,
    w_down,
    down_bias,
    ln2_gain,
    ln2_bias,
    cotangent,
):
    half = cotangent.shape[0]
    half_seqs = lengths.shape[0] // 2
    depth, width = w_out.shape[1], w_out.shape[0]
    me = lax.axis_index("tensor")
    pick = lax.dynamic_slice_in_dim
    x_own, x_far = pick(tokens, me * half, half, 0), pick(tokens, (1 - me) * half, half, 0)
    len_own = pick(lengths, me * half_seqs, half_seqs, 0)
    len_far = pick(lengths, (1 - me) * half_seqs, half_seqs, 0)
    w_all = jnp.concatenate((w_qkv[0], w_qkv[1], w_qkv[2]), axis=1)
    bias_pair = qv_bias.astype(f32)
    bias_all = jnp.concatenate((bias_pair[0], jnp.zeros((width,), f32), bias_pair[1]))

    qkv_far = (dot_of(x_far, w_all, 1, 0) + bias_all).astype(bf16)
    att_far, lse_far = attend(len_far, qkv_far)
    out_far = swap(dot_of(att_far, w_out, 1, 0).astype(bf16))
    qkv_own = (dot_of(x_own, w_all, 1, 0) + bias_all).astype(bf16)
    att_own, lse_own = attend(len_own, qkv_own)
    out_own = dot_of(att_own, w_out, 1, 0)
    gain1, gain2 = ln1_gain.astype(f32), ln2_gain.astype(f32)
    unit1, factor1 = normed(
        x_own.astype(f32) + (out_own + out_far.astype(f32) + out_bias.astype(f32))
    )
    hidden = unit1 * gain1 + ln1_bias.astype(f32)
    h_own = hidden.astype(bf16)
    h_far = swap(h_own)

    bias_in = in_bias.astype(f32)
    act_own, slope_own = lax.optimization_barrier(gelu_both(dot_of(h_own, w_in, 1, 0) + bias_in))
    act_far, slope_far = lax.optimization_barrier(gelu_both(dot_of(h_far, w_in, 1, 0) + bias_in))
    down_far = swap(dot_of(act_far, w_down, 1, 0).astype(bf16))
    down_own = dot_of(act_own, w_down, 1, 0)
    unit2, factor2 = normed(
        hidden + (down_own + down_far.astype(f32) + down_bias.astype(f32))
    )
    mixed_out = (unit2 * gain2 + ln2_bias.astype(f32)).astype(bf16)

    cot = cotangent.astype(f32)
    grad_gain2, grad_bias2 = jnp.sum(cot * unit2, axis=0), jnp.sum(cot, axis=0)
    grad_mid = norm_back(cot, gain2, unit2, factor2)
    grad_down_bias = jnp.sum(grad_mid, axis=0)
    gm_own = grad_mid.astype(bf16)
    gm_far = swap(gm_own)
    inner_own = dot_of(gm_own, w_down, 1, 1) * slope_own
    inner_far = dot_of(gm_far, w_down, 1, 1) * slope_far
    grad_in_bias = jnp.sum(inner_own, axis=0) + jnp.sum(inner_far, axis=0)
    gi_own, gi_far = inner_own.astype(bf16), inner_far.astype(bf16)
    gh_far = swap(dot_of(gi_far, w_in, 1, 1).astype(bf16))
    gh_own = dot_of(gi_own, w_in, 1, 1)
    g_down = (dot_of(act_own, gm_own, 0, 0) + dot_of(act_far, gm_far, 0, 0)).astype(bf16)
    g_in = (dot_of(h_own, gi_own, 0, 0) + dot_of(h_far, gi_far, 0, 0)).astype(bf16)

    grad_hidden = grad_mid + (gh_own + gh_far.astype(f32))
    grad_gain1, grad_bias1 = jnp.sum(grad_hidden * unit1, axis=0), jnp.sum(grad_hidden, axis=0)
    grad_first = norm_back(grad_hidden, gain1, unit1, factor1)
    grad_out_bias = jnp.sum(grad_first, axis=0)
    ga_own = grad_first.astype(bf16)
    ga_far = swap(ga_own)
    g_out = (dot_of(att_own, ga_own, 0, 0) + dot_of(att_far, ga_far, 0, 0)).astype(bf16)

    small = sum_small(
        jnp.concatenate(
            (grad_out_bias, grad_gain1, grad_bias1, grad_down_bias, grad_gain2, grad_bias2, grad_in_bias)
        ),
        size,
    )
    gatt_own = dot_of(ga_own, w_out, 1, 1).astype(bf16)
    gatt_far = dot_of(ga_far, w_out, 1, 1).astype(bf16)
    dq_own = attend_back(len_own, qkv_own, lse_own, gatt_own)
    dq_far = attend_back(len_far, qkv_far, lse_far, gatt_far)
    g_qkv = (dot_of(x_own, dq_own, 0, 0) + dot_of(x_far, dq_far, 0, 0)).astype(bf16)
    sums = jnp.sum(dq_own.astype(f32), axis=0) + jnp.sum(dq_far.astype(f32), axis=0)
    sums = sum_small(jnp.concatenate((sums[:width], sums[2 * width :])), size)
    ig_far = swap(dot_of(dq_far, w_all, 1, 1).astype(bf16))
    input_grad = dot_of(dq_own, w_all, 1, 1) + ig_far.astype(f32) + grad_first

    shared = small[: 6 * depth]
    shared = shared + swap(shared)
    shared = [shared[i * depth : (i + 1) * depth] for i in range(6)]
    g_down, g_in, g_out, g_qkv, sums, shared, small, input_grad = lax.optimization_barrier(
        (g_down, g_in, g_out, g_qkv, sums, shared, small, input_grad)
    )
    full_down, full_in, full_out, full_qkv = unpack(
        sum_packed(pack(g_down, g_in, g_out, g_qkv), size),
        (g_down.shape, g_in.shape, g_out.shape),
        w_qkv.shape,
    )
    return (
        mixed_out,
        input_grad,
        full_qkv,
        sums.reshape(2, width),
        full_out,
        shared[0],
        shared[1],
        shared[2],
        full_in,
        small[6 * depth :],
        full_down,
        shared[3],
        shared[4],
        shared[5],
    )


def solution(mesh):
    in_specs = (
        P("replica", None),
        P("replica"),
        P(None, None, "tensor"),
        P(None, "tensor"),
        P("tensor", None),
        P(),
        P(),
        P(),
        P(None, "tensor"),
        P("tensor"),
        P("tensor", None),
        P(),
        P(),
        P(),
        P(("replica", "tensor"), None),
    )
    out_specs = (
        P(("replica", "tensor"), None),
        P(("replica", "tensor"), None),
        P(None, None, "tensor"),
        P(None, "tensor"),
        P("tensor", None),
        P(),
        P(),
        P(),
        P(None, "tensor"),
        P("tensor"),
        P("tensor", None),
        P(),
        P(),
        P(),
    )
    return jax.shard_map(
        functools.partial(shards, mesh.shape["replica"]),
        mesh=mesh,
        in_specs=in_specs,
        out_specs=out_specs,
        check_vma=False,
    )
```
